32 devices in a mesh: groups: 2 (over y), tensor: 4 (over z), expert: 4 (over x, core).
Axes of the slice: x: 2, y: 2, z: 4, core: 2. Of those that a mesh axis runs over, the one named last changes fastest.
Arguments:
- tokens: bfloat16 [1024, 3072], P(('groups', 'expert'), 'tensor'), parts along dimension 0, may hold values from -6 to 6
- routes: int32 [1024, 2], P(('groups', 'expert')), parts along dimension 0, may hold values from 0 to 3, all different within a row; in each aligned block of 128 rows (0 to 127, 128 to 255, ...) at most 72 rows name the same one
- gates: float32 [1024, 2], P(('groups', 'expert')), parts along dimension 0, may hold values from 0.25 to 1
- w_gate: bfloat16 [4, 3072, 8192], P('expert', None, 'tensor'), may hold values from -0.109375 to 0.109375
- w_up: bfloat16 [4, 3072, 8192], P('expert', None, 'tensor'), may hold values from -0.109375 to 0.109375
- w_down: bfloat16 [4, 8192, 3072], P('expert', 'tensor'), may hold values from -0.09375 to 0.09375
Outputs:
- mixed: bfloat16 [1024, 3072], P(('groups', 'expert'), 'tensor'), parts along dimension 0
The draws below stay inside these ranges and needn't reach their ends.
There are 2 independent parts, one for each index of `groups`. The reference program is written for one: setup_inputs(seed, part) draws one part's arguments, and reference() takes and returns one part's arrays. A program takes and returns all parts, laid end to end along the dimension named above; an argument that names none is the same for every part. Nothing has to cross between parts.
Inputs may be any that keep to these rules, and one draw needn't show every extreme that they name: `routes`: each row names two different experts. Among the rows of one index of expert no expert is named more than 72 times, a bound that some block reaches.
All inputs are finite; a program needn't handle non-finite values.
Results may differ from the reference program's by a relative error of at most 0.012.
Values may be sent and summed in bfloat16 or wider, within the bound.
A program may use at most 128 MiB of HBM per device.

```python
import math
import jax
import jax.numpy as jnp
import numpy as np
from jax import lax

D = 3072
FF = 8192
EXPERTS = 4
TOK_DEV = 128
CAP = 72
TOKENS = 512
COLS = 2048
N_TENSOR = 4
N_EXPERT = 4


def raised(drawn, own_key, source, target, shards_of, factor):
    owner, partner = [(jnp.arange(drawn.shape[dim]) // (drawn.shape[dim] // shards_of)).reshape([-1 if axis == dim else 1 for axis in range(drawn.ndim)]) for dim in (source, target)]
    chosen = jax.random.permutation(own_key, shards_of)[partner]
    strong = (owner == chosen) | (owner == (partner + shards_of // 2) % shards_of)
    return jnp.where(strong, factor * drawn, drawn)


def block_scale(key, dims, split, low, largest):
    level, own = 1.0, jax.random.fold_in(key, 6)
    for dim, blocks in split:
        steps = jnp.exp(jax.random.uniform(jax.random.fold_in(own, dim), (blocks,), jnp.float32, low / len(split), largest / len(split)))
        level = level * jnp.repeat(steps, dims[dim] // blocks).reshape([-1 if axis == dim else 1 for axis in range(len(dims))])
    return level


def routed_block(key, own, number, rows, count, top, reach, lean):
    order = jax.random.permutation(key, count)
    packed, common = shares(count, rows * top, reach, lean, True), shares(count, rows * top, reach, lean, False)
    places = jnp.arange(count)

    def named(tallies, turn):
        used = int((tallies > 0).sum())
        fixed = max(1, used // 4)
        shifted = fixed + (places - fixed + turn * (used - fixed)) % max(1, count - fixed)
        return jnp.zeros((count,), jnp.int32).at[order[jnp.where(places < fixed, places, shifted)]].set(jnp.asarray(tallies, jnp.int32))

    tallies = jnp.where(number % 4 == 0, named(packed, number // 4), named(common, number - number // 4 - 1))
    mixed = jax.random.permutation(jax.random.fold_in(own, 3), count)
    source_of, sink = mixed[0:count // 2 * 2:2], mixed[1:count // 2 * 2:2]
    slack = jnp.minimum(tallies[source_of] - 1, reach - tallies[sink]) // 2
    slack = jnp.where((source_of == order[0]) | (sink == order[0]) | (tallies[sink] == 0), 0, jnp.maximum(slack, 0))
    shifted = jax.random.randint(jax.random.fold_in(own, 4), (count // 2,), 0, 1 << 20) % (slack + 1)
    tallies = tallies.at[source_of].add(-shifted).at[sink].add(shifted)
    members = jnp.searchsorted(jnp.cumsum(tallies), jnp.arange(rows * top), side="right").astype(jnp.int32)
    table = members.reshape(top, rows).T
    table = table[jax.random.permutation(jax.random.fold_in(own, 1), rows)]
    turn = jax.random.randint(jax.random.fold_in(own, 2), (rows, 1), 0, top)
    return jnp.take_along_axis(table, (jnp.arange(top)[None, :] + turn) % top, axis=1)


def shares(amount, total, reach, skew, full):
    loads = [(1 << 20) // math.isqrt(rank ** skew) + 1 for rank in range(1, amount + 1)]
    largest = reach if full else min(reach, max(-(-total // amount), total * loads[0] // sum(loads)))
    least = 1 if total - largest >= amount - 1 else 0
    counts, surplus = [largest] + [least] * (amount - 1), total - largest - least * (amount - 1)
    while surplus > 0:
        candidates = [i for i in range(1, amount) if counts[i] < largest] or [i for i in range(1, amount) if counts[i] < reach]
        mass, left = sum([loads[i] for i in candidates]), surplus
        for i in candidates:
            more = min(reach - counts[i], max(1, left * loads[i] // mass), surplus)
            counts[i] = counts[i] + more
            surplus = surplus - more
    return np.array(counts)


def scatter_about(stream_key, dims, spread, most, split=(), kind=jnp.bfloat16):
    level = block_scale(stream_key, dims, split, -0.22, 0.18) if split else 1.0
    values = jax.random.normal(stream_key, dims, jnp.float32) * spread * level
    return jnp.minimum(jnp.maximum(values, -most), most).astype(kind)


def heavy_noise(stream_key, shape, deviation, most, split, heavy, kind=jnp.bfloat16):
    entries = deviation * jax.random.normal(stream_key, shape, jnp.float32)
    if split:
        entries = entries * block_scale(stream_key, shape, split, -0.22, 0.18)
    return jnp.clip(raised(entries, jax.random.fold_in(stream_key, 3), *heavy), -most, most).astype(kind)


def setup_inputs(seed: int = 0, part: int = 0) -> dict:
    key_of = jax.random.split(jax.random.key(seed), 7)
    part_splits = jax.random.split(jax.random.fold_in(key_of[6], part), 7)
    tokens = scatter_about(part_splits[0], (TOKENS, D), 1.0, 6.0, ((0, 4), (1, 4)))
    routes_keys = jax.random.split(jax.random.fold_in(part_splits[1], 1), TOKENS // TOK_DEV)
    routes_turns = jax.random.permutation(jax.random.fold_in(part_splits[1], 3), TOKENS // TOK_DEV)
    routes = jax.vmap(lambda own, number: routed_block(jax.random.fold_in(part_splits[1], 2), own, number, TOK_DEV, EXPERTS, 2, CAP, 2))(routes_keys, routes_turns).reshape((TOKENS, 2))
    gates = jnp.clip(0.25 + 0.75 * jax.random.uniform(part_splits[2], (TOKENS, 2), jnp.float32) ** block_scale(part_splits[2], (TOKENS, 2), ((0, 4),), -0.2, 0.2), 0.25, 1.0)
    w_gate = scatter_about(key_of[3], (EXPERTS, D, FF), D ** -0.5, 0.109375, ((0, 4), (2, 4)))
    w_up = scatter_about(key_of[4], (EXPERTS, D, FF), D ** -0.5, 0.109375, ((0, 4), (2, 4)))
    w_down = heavy_noise(key_of[5], (EXPERTS, FF, D), FF ** -0.5, 0.09375, ((0, 4), (1, 4)), (1, 2, 4, 2.0))
    return {"tokens": tokens, "routes": routes, "gates": gates, "w_gate": w_gate, "w_up": w_up, "w_down": w_down}


def reference(tokens, routes, gates, w_gate, w_up, w_down):
    limit = min(N_EXPERT * CAP, TOKENS)
    mixed = jnp.zeros((TOKENS, D), jnp.float32)
    for expert in range(EXPERTS):
        hits = routes == expert
        chosen = jnp.any(hits, axis=1)
        rows = jnp.nonzero(chosen, size=limit, fill_value=0)[0].astype(jnp.int32)
        valid = jnp.arange(limit, dtype=jnp.int32) < jnp.sum(chosen.astype(jnp.int32))
        weight = jnp.sum(jnp.where(hits, gates, jnp.zeros_like(gates)), axis=1)[rows]
        picked = tokens[rows]
        gate = jnp.dot(picked, w_gate[expert], preferred_element_type=jnp.float32)
        upper = jnp.dot(picked, w_up[expert], preferred_element_type=jnp.float32)
        hidden = (jax.nn.silu(gate) * upper).astype(jnp.bfloat16)
        panel_all = w_down[expert]

        def add_block(total, index):
            block = lax.dynamic_slice_in_dim(hidden, index * COLS, COLS, 1)
            panel = lax.dynamic_slice_in_dim(panel_all, index * COLS, COLS, 0)
            part = jnp.dot(block, panel, preferred_element_type=jnp.float32).astype(jnp.bfloat16)
            part = lax.optimization_barrier(part)
            return total + part.astype(jnp.float32), None

        total, _ = lax.scan(add_block, jnp.zeros((limit, D), jnp.float32), jnp.arange(N_TENSOR, dtype=jnp.int32))
        result = lax.optimization_barrier(total.astype(jnp.bfloat16)).astype(jnp.float32)
        contribution = jnp.where(valid[:, None], weight[:, None] * result, jnp.zeros_like(result))
        mixed = mixed.at[rows].add(contribution)
    return mixed.astype(jnp.bfloat16)
```

```python
import jax
import jax.numpy as jnp
from jax import lax
from jax.experimental import pallas as pl
from jax.experimental.pallas import tpu as pltpu
from jax.sharding import PartitionSpec as P

CAP = 72
MESH = pl.DeviceIdType.MESH


row_tile = 128


def route_ranks(flat, experts):
    onehot = (flat[:, None] == jnp.arange(experts, dtype=jnp.int32)[None, :]).astype(jnp.int32)
    return jnp.sum((jnp.cumsum(onehot, axis=0) - 1) * onehot, axis=1)


def tile_terms(block, gate_panel, up_panel, down_panel):
    gate = jnp.dot(block, gate_panel, preferred_element_type=jnp.float32)
    upper = jnp.dot(block, up_panel, preferred_element_type=jnp.float32)
    hidden = (jax.nn.silu(gate) * upper).astype(jnp.bfloat16)
    return jnp.dot(hidden, down_panel, preferred_element_type=jnp.float32)


def expert_rows(rows, live, gate_panel, up_panel, down_panel):
    total = rows.shape[0]
    width = down_panel.shape[1]

    def step(index, acc):
        block = lax.dynamic_slice_in_dim(rows, index * row_tile, row_tile, 0)
        product = tile_terms(block, gate_panel, up_panel, down_panel)
        return lax.dynamic_update_slice_in_dim(acc, product, index * row_tile, 0)

    tiles = (live + row_tile - 1) // row_tile
    return lax.fori_loop(0, tiles, step, jnp.zeros((total, width), jnp.float32))


def compact_rows(arrived, incoming, offsets, padded):
    experts, capacity, width = arrived.shape
    position = jnp.arange(experts * capacity, dtype=jnp.int32)
    source = position // capacity
    within = position % capacity
    live_row = within < incoming[source]
    dest = jnp.where(live_row, offsets[source] + within, padded)
    flat_rows = arrived.reshape(experts * capacity, width)
    return jnp.zeros((padded, width), arrived.dtype).at[dest].set(flat_rows, mode="drop")


def per_device(tokens, routes, gates, w_gate, w_up, w_down):
    experts = lax.axis_size("expert")
    me = lax.axis_index("expert")
    tok = routes.shape[0]
    slice_width = tokens.shape[1]
    slots = experts * CAP
    padded = (slots + row_tile - 1) // row_tile * row_tile
    table = lax.all_gather(routes, "expert", axis=0, tiled=True)
    every_flat = table.reshape(-1)
    source_of = jnp.arange(every_flat.shape[0], dtype=jnp.int32) // (2 * tok)
    pair_index = source_of * experts + every_flat
    loads = jnp.sum(
        (pair_index[:, None] == jnp.arange(experts * experts, dtype=jnp.int32)[None, :]).astype(
            jnp.int32
        ),
        axis=0,
    ).reshape(experts, experts)
    flat = routes.reshape(-1)
    ranks = route_ranks(flat, experts)
    token_of = jnp.arange(2 * tok, dtype=jnp.int32) // 2
    incoming = loads[:, me]
    offsets = jnp.cumsum(incoming) - incoming
    live = jnp.sum(incoming)
    target = flat * CAP + ranks
    chosen = tokens[token_of]
    width = chosen.shape[1]
    outgoing = (
        jnp.zeros((slots, width), jnp.bfloat16)
        .at[target]
        .set(chosen, mode="drop")
        .reshape(experts, CAP, width)
    )
    arrived = lax.all_to_all(outgoing, "expert", split_axis=0, concat_axis=0, tiled=True)
    stacked = compact_rows(arrived, incoming, offsets, padded)
    stacked = lax.all_gather(stacked, "tensor", axis=1, tiled=True)
    terms = expert_rows(stacked, live, w_gate[0], w_up[0], w_down[0])
    summed = lax.psum_scatter(terms.astype(jnp.bfloat16), "tensor", scatter_dimension=1, tiled=True)
    position = jnp.arange(slots, dtype=jnp.int32)
    source = position // CAP
    within = position % CAP
    live_row = within < incoming[source]
    fetch = jnp.clip(offsets[source] + within, 0, padded - 1)
    restored = jnp.where(
        live_row[:, None], summed[fetch], jnp.zeros((slots, slice_width), jnp.bfloat16)
    )
    returned = lax.all_to_all(
        restored.reshape(experts, CAP, slice_width),
        "expert",
        split_axis=0,
        concat_axis=0,
        tiled=True,
    ).reshape(slots, slice_width)
    picked = returned[jnp.clip(target, 0, slots - 1)]
    weighted = picked.astype(jnp.float32).reshape(tok, 2, slice_width) * gates[:, :, None]
    return jnp.sum(weighted, axis=1).astype(jnp.bfloat16)


def pair_steps(z):
    return (z, z + 1 - 2 * (z % 2), (z + 2) % 4, 3 - z)


def layer_kernel(
    meta_in, tok_in, gate_hbm, up_hbm, down_hbm, out,
    toks, meta, gate_w, up_w, down_w, gate_acc, up_acc, rows_buf, hid, pick, place, scale, terms,
    outs, core_in, x_out, x_in, z_out, z_in,
    w_sem, meta_send, meta_recv, z_send, x_send, core_send, tok_recv,
    rc_send, rc_recv, rx_send, rx_recv, rz_send, rz_recv,
):
    e = lax.axis_index("expert")
    z = lax.axis_index("tensor")
    x = e // 2
    c = e % 2
    core_e = 2 * x + 1 - c
    x_e = 2 * (1 - x) + c
    diag_e = 2 * (1 - x) + 1 - c
    zs = pair_steps(z)
    tok, width = tok_in.shape
    slots = pick.shape[0]
    every = pick.shape[1]
    hidden = hid.shape[1]

    weight_copies = []
    for k in range(4):
        cut = pl.ds(pl.multiple_of(zs[k] * width, width), width)
        weight_copies.append(
            (
                pltpu.make_async_copy(gate_hbm.at[cut, :], gate_w.at[k], w_sem.at[k]),
                pltpu.make_async_copy(up_hbm.at[cut, :], up_w.at[k], w_sem.at[4 + k]),
                pltpu.make_async_copy(down_hbm.at[:, cut], down_w.at[k], w_sem.at[8 + k]),
            )
        )
    for k in range(4):
        weight_copies[k][0].start()
        weight_copies[k][1].start()
    for k in (3, 2, 1, 0):
        weight_copies[k][2].start()

    barrier = pltpu.get_barrier_semaphore()
    for other in (core_e, x_e, diag_e):
        pl.semaphore_signal(barrier, inc=1, device_id={"expert": other}, device_id_type=MESH)
    for k in (1, 2, 3):
        pl.semaphore_signal(barrier, inc=1, device_id={"tensor": zs[k]}, device_id_type=MESH)
    pl.semaphore_wait(barrier, 6)

    sends = []

    def send(src, dst, s_sem, r_sem, where):
        copy = pltpu.make_async_remote_copy(
            src_ref=src, dst_ref=dst, send_sem=s_sem, recv_sem=r_sem,
            device_id=where, device_id_type=MESH,
        )
        copy.start()
        sends.append(copy)

    def arrival(ref, sem):
        pltpu.make_async_copy(ref, ref, sem).wait()

    for i, other in enumerate((x_e, core_e, diag_e)):
        send(meta_in, meta.at[e], meta_send.at[i], meta_recv.at[e], {"expert": other})
    own = z * 4 + e
    send(tok_in, toks.at[own], x_send.at[0], tok_recv.at[own], {"expert": x_e})
    for k in (1, 2, 3):
        send(tok_in, toks.at[own], z_send.at[k - 1], tok_recv.at[own], {"tensor": zs[k]})
    send(tok_in, toks.at[own], core_send.at[0], tok_recv.at[own], {"expert": core_e})
    toks[own] = tok_in[...]
    meta[e] = meta_in[...]

    def forward_z(k):
        block = zs[k] * 4 + e
        arrival(toks.at[block], tok_recv.at[block])
        send(toks.at[block], toks.at[block], x_send.at[k], tok_recv.at[block], {"expert": x_e})
        send(toks.at[block], toks.at[block], core_send.at[k], tok_recv.at[block], {"expert": core_e})

    def forward_x(k):
        block = zs[k] * 4 + x_e
        arrival(toks.at[block], tok_recv.at[block])
        send(toks.at[block], toks.at[block], core_send.at[4 + k], tok_recv.at[block], {"expert": core_e})

    for other in (x_e, core_e, diag_e):
        arrival(meta.at[other], meta_recv.at[other])

    own_row = lax.broadcasted_iota(jnp.int32, (8, tok), 0) == e
    weight = jnp.concatenate(
        [jnp.sum(jnp.where(own_row, meta[s], 0.0), axis=0, keepdims=True) for s in range(4)], axis=1
    )
    live = weight > 0.0
    ones = jnp.broadcast_to(jnp.where(live, 1.0, 0.0), (16, every)).astype(jnp.bfloat16)
    before = jnp.where(
        lax.broadcasted_iota(jnp.int32, (every, every), 0)
        < lax.broadcasted_iota(jnp.int32, (every, every), 1),
        1.0,
        0.0,
    ).astype(jnp.bfloat16)
    rank = jnp.dot(ones, before, preferred_element_type=jnp.float32)[0:1]
    key = jnp.where(live, rank, -1.0)
    row_hit = lax.broadcasted_iota(jnp.int32, (slots, every), 0).astype(jnp.float32) == key
    pick[...] = jnp.where(row_hit, 1.0, 0.0).astype(jnp.bfloat16)
    scale[...] = jnp.broadcast_to(
        jnp.sum(jnp.where(row_hit, weight, 0.0), axis=1, keepdims=True), scale.shape
    )
    column = jnp.transpose(jnp.broadcast_to(key, (128, every)))[:, 0:1]
    padded = place.shape[1]
    place[...] = jnp.where(
        lax.broadcasted_iota(jnp.int32, (every, padded), 1).astype(jnp.float32) == column, 1.0, 0.0
    ).astype(jnp.bfloat16)
    terms[slots:, :] = jnp.zeros((padded - slots, width), jnp.bfloat16)

    tile = 512

    def up_step(k):
        weight_copies[k][0].wait()
        weight_copies[k][1].wait()
        blocks = toks[pl.ds(zs[k] * 4, 4)].reshape(every, width)
        rows_buf[...] = jnp.dot(
            pick[...], blocks, preferred_element_type=jnp.float32
        ).astype(jnp.bfloat16)

        @pl.loop(0, hidden // tile)
        def _(i):
            cols = pl.ds(pl.multiple_of(i * tile, tile), tile)
            rows = rows_buf[...]
            gate = jnp.dot(rows, gate_w[k, :, cols], preferred_element_type=jnp.float32)
            upper = jnp.dot(rows, up_w[k, :, cols], preferred_element_type=jnp.float32)
            if k > 0:
                gate = gate + gate_acc[:, cols]
                upper = upper + up_acc[:, cols]
            if k < 3:
                gate_acc[:, cols] = gate
                up_acc[:, cols] = upper
            else:
                hid[:, cols] = (gate / (1.0 + jnp.exp(-gate)) * upper).astype(jnp.bfloat16)

    def core_arrivals(k):
        for other in (core_e, diag_e):
            block = zs[k] * 4 + other
            arrival(toks.at[block], tok_recv.at[block])

    for k in range(4):
        if k < 3:
            forward_z(k + 1)
        forward_x(k)
        core_arrivals(k)
        up_step(k)

    down_tile = 256

    def down_step(k):
        weight_copies[k][2].wait()

        @pl.loop(0, width // down_tile)
        def _(i):
            cols = pl.ds(pl.multiple_of(i * down_tile, down_tile), down_tile)
            product = jnp.dot(hid[...], down_w[k, :, cols], preferred_element_type=jnp.float32)
            terms[0:slots, cols] = (product * scale[:, 0:1]).astype(jnp.bfloat16)
            spread = jnp.dot(place[...], terms[:, cols], preferred_element_type=jnp.float32)
            outs[k, :, :, cols] = spread.astype(jnp.bfloat16).reshape(4, tok, down_tile)

        for i, there in enumerate((1 - x, x)):
            send(
                outs.at[k, 2 * there + 1 - c], core_in.at[k, i],
                rc_send.at[2 * k + i], rc_recv.at[2 * k + i], {"expert": core_e},
            )

    def core_step(k):
        arrival(core_in.at[k, 0], rc_recv.at[2 * k])
        x_out[k] = (
            outs[k, x_e].astype(jnp.float32) + core_in[k, 0].astype(jnp.float32)
        ).astype(jnp.bfloat16)
        send(x_out.at[k], x_in.at[k], rx_send.at[k], rx_recv.at[k], {"expert": x_e})

    def x_step(k):
        arrival(core_in.at[k, 1], rc_recv.at[2 * k + 1])
        arrival(x_in.at[k], rx_recv.at[k])
        total = (
            outs[k, e].astype(jnp.float32)
            + core_in[k, 1].astype(jnp.float32)
            + x_in[k].astype(jnp.float32)
        )
        if k > 0:
            z_out[k - 1] = total.astype(jnp.bfloat16)
            send(
                z_out.at[k - 1], z_in.at[k - 1], rz_send.at[k - 1], rz_recv.at[k - 1],
                {"tensor": zs[k]},
            )
            return None
        return total

    down_step(3)
    core_step(3)
    down_step(2)
    core_step(2)
    x_step(3)
    down_step(1)
    core_step(1)
    down_step(0)
    core_step(0)
    x_step(2)
    x_step(1)
    total = x_step(0)
    for k in (3, 2, 1):
        arrival(z_in.at[k - 1], rz_recv.at[k - 1])
        total = total + z_in[k - 1].astype(jnp.float32)
    out[...] = total.astype(jnp.bfloat16)
    for copy in sends:
        copy.wait_send()


def per_device_fused(tokens, routes, gates, w_gate, w_up, w_down):
    tok, width = tokens.shape
    model, hidden = w_gate.shape[1:]
    experts = lax.axis_size("expert")
    slots = experts * CAP
    padded = (slots + 127) // 128 * 128
    every = experts * tok
    named = jnp.arange(8, dtype=jnp.int32)[:, None]
    meta = jnp.where(routes[:, 0][None] == named, gates[:, 0][None], 0.0) + jnp.where(
        routes[:, 1][None] == named, gates[:, 1][None], 0.0
    )
    vmem = pl.BlockSpec(memory_space=pltpu.VMEM)
    hbm = pl.BlockSpec(memory_space=pl.ANY)
    bf, f32, dma = jnp.bfloat16, jnp.float32, pltpu.SemaphoreType.DMA
    return pl.pallas_call(
        layer_kernel,
        out_shape=jax.ShapeDtypeStruct((tok, width), bf),
        in_specs=[vmem, vmem, hbm, hbm, hbm],
        out_specs=vmem,
        scratch_shapes=[
            pltpu.VMEM((4 * experts, tok, width), bf),
            pltpu.VMEM((experts, 8, tok), f32),
            pltpu.VMEM((4, width, hidden), bf),
            pltpu.VMEM((4, width, hidden), bf),
            pltpu.VMEM((4, hidden, width), bf),
            pltpu.VMEM((slots, hidden), f32),
            pltpu.VMEM((slots, hidden), f32),
            pltpu.VMEM((slots, width), bf),
            pltpu.VMEM((slots, hidden), bf),
            pltpu.VMEM((slots, every), bf),
            pltpu.VMEM((every, padded), bf),
            pltpu.VMEM((slots, 128), f32),
            pltpu.VMEM((padded, width), bf),
            pltpu.VMEM((4, experts, tok, width), bf),
            pltpu.VMEM((4, 2, tok, width), bf),
            pltpu.VMEM((4, tok, width), bf),
            pltpu.VMEM((4, tok, width), bf),
            pltpu.VMEM((3, tok, width), bf),
            pltpu.VMEM((3, tok, width), bf),
            dma((12,)), dma((3,)), dma((experts,)), dma((3,)), dma((4,)), dma((8,)),
            dma((4 * experts,)),
            dma((8,)), dma((8,)), dma((4,)), dma((4,)), dma((3,)), dma((3,)),
        ],
        compiler_params=pltpu.CompilerParams(
            collective_id=0, has_side_effects=True, vmem_limit_bytes=62 * 1024 * 1024
        ),
        cost_estimate=pl.CostEstimate(
            flops=6 * slots * model * hidden,
            bytes_accessed=6 * model * hidden,
            transcendentals=slots * hidden,
        ),
    )(meta, tokens, w_gate[0], w_up[0], w_down[0])


def solution(mesh):
    in_specs = (
        P(("groups", "expert"), "tensor"),
        P(("groups", "expert"), None),
        P(("groups", "expert"), None),
        P("expert", None, "tensor"),
        P("expert", None, "tensor"),
        P("expert", "tensor", None),
    )
    out_specs = P(("groups", "expert"), "tensor")
    fused = mesh.shape["tensor"] == 4 and mesh.shape["expert"] == 4
    return jax.shard_map(
        per_device_fused if fused else per_device,
        mesh=mesh, in_specs=in_specs, out_specs=out_specs, check_vma=False,
    )
```

```python
import jax
import jax.numpy as jnp
from jax import lax
from jax.experimental import pallas as pl
from jax.experimental.pallas import tpu as pltpu
from jax.sharding import PartitionSpec as P

CAP = 72
MESH = pl.DeviceIdType.MESH


row_tile = 128


def route_ranks(flat, experts):
    onehot = (flat[:, None] == jnp.arange(experts, dtype=jnp.int32)[None, :]).astype(jnp.int32)
    return jnp.sum((jnp.cumsum(onehot, axis=0) - 1) * onehot, axis=1)


def tile_terms(block, gate_panel, up_panel, down_panel):
    gate = jnp.dot(block, gate_panel, preferred_element_type=jnp.float32)
    upper = jnp.dot(block, up_panel, preferred_element_type=jnp.float32)
    hidden = (jax.nn.silu(gate) * upper).astype(jnp.bfloat16)
    return jnp.dot(hidden, down_panel, preferred_element_type=jnp.float32)


def expert_rows(rows, live, gate_panel, up_panel, down_panel):
    total = rows.shape[0]
    width = down_panel.shape[1]

    def step(index, acc):
        block = lax.dynamic_slice_in_dim(rows, index * row_tile, row_tile, 0)
        product = tile_terms(block, gate_panel, up_panel, down_panel)
        return lax.dynamic_update_slice_in_dim(acc, product, index * row_tile, 0)

    tiles = (live + row_tile - 1) // row_tile
    return lax.fori_loop(0, tiles, step, jnp.zeros((total, width), jnp.float32))


def compact_rows(arrived, incoming, offsets, padded):
    experts, capacity, width = arrived.shape
    position = jnp.arange(experts * capacity, dtype=jnp.int32)
    source = position // capacity
    within = position % capacity
    live_row = within < incoming[source]
    dest = jnp.where(live_row, offsets[source] + within, padded)
    flat_rows = arrived.reshape(experts * capacity, width)
    return jnp.zeros((padded, width), arrived.dtype).at[dest].set(flat_rows, mode="drop")


def per_device(tokens, routes, gates, w_gate, w_up, w_down):
    experts = lax.axis_size("expert")
    me = lax.axis_index("expert")
    tok = routes.shape[0]
    slice_width = tokens.shape[1]
    slots = experts * CAP
    padded = (slots + row_tile - 1) // row_tile * row_tile
    table = lax.all_gather(routes, "expert", axis=0, tiled=True)
    every_flat = table.reshape(-1)
    source_of = jnp.arange(every_flat.shape[0], dtype=jnp.int32) // (2 * tok)
    pair_index = source_of * experts + every_flat
    loads = jnp.sum(
        (pair_index[:, None] == jnp.arange(experts * experts, dtype=jnp.int32)[None, :]).astype(
            jnp.int32
        ),
        axis=0,
    ).reshape(experts, experts)
    flat = routes.reshape(-1)
    ranks = route_ranks(flat, experts)
    token_of = jnp.arange(2 * tok, dtype=jnp.int32) // 2
    incoming = loads[:, me]
    offsets = jnp.cumsum(incoming) - incoming
    live = jnp.sum(incoming)
    target = flat * CAP + ranks
    chosen = tokens[token_of]
    width = chosen.shape[1]
    outgoing = (
        jnp.zeros((slots, width), jnp.bfloat16)
        .at[target]
        .set(chosen, mode="drop")
        .reshape(experts, CAP, width)
    )
    arrived = lax.all_to_all(outgoing, "expert", split_axis=0, concat_axis=0, tiled=True)
    stacked = compact_rows(arrived, incoming, offsets, padded)
    stacked = lax.all_gather(stacked, "tensor", axis=1, tiled=True)
    terms = expert_rows(stacked, live, w_gate[0], w_up[0], w_down[0])
    summed = lax.psum_scatter(terms.astype(jnp.bfloat16), "tensor", scatter_dimension=1, tiled=True)
    position = jnp.arange(slots, dtype=jnp.int32)
    source = position // CAP
    within = position % CAP
    live_row = within < incoming[source]
    fetch = jnp.clip(offsets[source] + within, 0, padded - 1)
    restored = jnp.where(
        live_row[:, None], summed[fetch], jnp.zeros((slots, slice_width), jnp.bfloat16)
    )
    returned = lax.all_to_all(
        restored.reshape(experts, CAP, slice_width),
        "expert",
        split_axis=0,
        concat_axis=0,
        tiled=True,
    ).reshape(slots, slice_width)
    picked = returned[jnp.clip(target, 0, slots - 1)]
    weighted = picked.astype(jnp.float32).reshape(tok, 2, slice_width) * gates[:, :, None]
    return jnp.sum(weighted, axis=1).astype(jnp.bfloat16)


def near_to_far(z):
    half = z // 2
    return (z, z + 1 - 2 * (z % 2), 2 - half, 3 - 3 * half)


def layer_kernel(
    routes_in, gates_in, tok_in, gate_hbm, up_hbm, down_hbm, out,
    toks, meta_in, meta, gate_w, up_w, down_w, gate_acc, up_acc, rows_buf, hid, pick, place, scale, terms,
    outs, core_in, x_out, x_in, z_out, z_in,
    w_sem, meta_send, meta_recv, z_send, x_send, core_send, tok_recv,
    rc_send, rc_recv, rx_send, rx_recv, rz_send, rz_recv,
):
    e = lax.axis_index("expert")
    z = lax.axis_index("tensor")
    x = e // 2
    c = e % 2
    core_e = 2 * x + 1 - c
    x_e = 2 * (1 - x) + c
    diag_e = 2 * (1 - x) + 1 - c
    zs = near_to_far(z)
    outer, inner = zs[1], 3 - z
    middle = z % 3 > 0
    end = z % 3 == 0
    tok, width = tok_in.shape
    slots = pick.shape[0]
    every = pick.shape[1]
    hidden = hid.shape[1]

    named = lax.broadcasted_iota(jnp.int32, (8, tok), 0)
    meta_in[...] = jnp.where(routes_in[0:1, :] == named, gates_in[0:1, :], 0.0) + jnp.where(
        routes_in[1:2, :] == named, gates_in[1:2, :], 0.0
    )
    weight_copies = []
    for k in range(4):
        cut = pl.ds(pl.multiple_of(zs[k] * width, width), width)
        weight_copies.append(
            (
                pltpu.make_async_copy(gate_hbm.at[cut, :], gate_w.at[k], w_sem.at[k]),
                pltpu.make_async_copy(up_hbm.at[cut, :], up_w.at[k], w_sem.at[4 + k]),
                pltpu.make_async_copy(down_hbm.at[:, cut], down_w.at[k], w_sem.at[8 + k]),
            )
        )
    for k in range(4):
        weight_copies[k][0].start()
        weight_copies[k][1].start()
    for k in (3, 2, 1, 0):
        weight_copies[k][2].start()

    barrier = pltpu.get_barrier_semaphore()
    for other in (core_e, x_e, diag_e):
        pl.semaphore_signal(barrier, inc=1, device_id={"expert": other}, device_id_type=MESH)
    pl.semaphore_signal(barrier, inc=1, device_id={"tensor": outer}, device_id_type=MESH)

    @pl.when(middle)
    def _():
        pl.semaphore_signal(barrier, inc=1, device_id={"tensor": inner}, device_id_type=MESH)
        pl.semaphore_wait(barrier, 5)

    @pl.when(end)
    def _():
        pl.semaphore_wait(barrier, 4)


    sends = []

    def send(src, dst, s_sem, r_sem, where, keep=True):
        copy = pltpu.make_async_remote_copy(
            src_ref=src, dst_ref=dst, send_sem=s_sem, recv_sem=r_sem,
            device_id=where, device_id_type=MESH,
        )
        copy.start()
        if keep:
            sends.append(copy)
        return copy

    def arrival(ref, sem):
        pltpu.make_async_copy(ref, ref, sem).wait()

    for i, other in enumerate((x_e, core_e, diag_e)):
        send(meta_in, meta.at[e], meta_send.at[i], meta_recv.at[e], {"expert": other})
    own = z * 4 + e
    send(tok_in, toks.at[own], x_send.at[0], tok_recv.at[own], {"expert": x_e})
    send(tok_in, toks.at[own], z_send.at[0], tok_recv.at[own], {"tensor": outer})

    @pl.when(middle)
    def _():
        send(tok_in, toks.at[own], z_send.at[1], tok_recv.at[own], {"tensor": inner}, False)

    send(tok_in, toks.at[own], core_send.at[0], tok_recv.at[own], {"expert": core_e})
    toks[own] = tok_in[...]
    meta[e] = meta_in[...]

    def block_of(k):
        return zs[k] * 4 + e

    def land_z(k):
        block = block_of(k)
        arrival(toks.at[block], tok_recv.at[block])

    def pass_on(k):
        block = block_of(k)
        there = inner if k == 1 else outer
        return pltpu.make_async_remote_copy(
            src_ref=toks.at[block], dst_ref=toks.at[block],
            send_sem=z_send.at[k + 1], recv_sem=tok_recv.at[block],
            device_id={"tensor": there}, device_id_type=MESH,
        )

    def spread_z(k):
        block = block_of(k)
        send(toks.at[block], toks.at[block], x_send.at[k], tok_recv.at[block], {"expert": x_e})
        send(toks.at[block], toks.at[block], core_send.at[k], tok_recv.at[block], {"expert": core_e})

    def forward_x(k):
        block = zs[k] * 4 + x_e
        arrival(toks.at[block], tok_recv.at[block])
        send(toks.at[block], toks.at[block], core_send.at[4 + k], tok_recv.at[block], {"expert": core_e})

    for other in (x_e, core_e, diag_e):
        arrival(meta.at[other], meta_recv.at[other])

    own_row = lax.broadcasted_iota(jnp.int32, (8, tok), 0) == e
    weight = jnp.concatenate(
        [jnp.sum(jnp.where(own_row, meta[s], 0.0), axis=0, keepdims=True) for s in range(4)], axis=1
    )
    live = weight > 0.0
    ones = jnp.broadcast_to(jnp.where(live, 1.0, 0.0), (16, every)).astype(jnp.bfloat16)
    before = jnp.where(
        lax.broadcasted_iota(jnp.int32, (every, every), 0)
        < lax.broadcasted_iota(jnp.int32, (every, every), 1),
        1.0,
        0.0,
    ).astype(jnp.bfloat16)
    rank = jnp.dot(ones, before, preferred_element_type=jnp.float32)[0:1]
    key = jnp.where(live, rank, -1.0)
    row_hit = lax.broadcasted_iota(jnp.int32, (slots, every), 0).astype(jnp.float32) == key
    pick[...] = jnp.where(row_hit, 1.0, 0.0).astype(jnp.bfloat16)
    scale[...] = jnp.broadcast_to(
        jnp.sum(jnp.where(row_hit, weight, 0.0), axis=1, keepdims=True), scale.shape
    )
    column = jnp.transpose(jnp.broadcast_to(key, (128, every)))[:, 0:1]
    padded = place.shape[1]
    place[...] = jnp.where(
        lax.broadcasted_iota(jnp.int32, (every, padded), 1).astype(jnp.float32) == column, 1.0, 0.0
    ).astype(jnp.bfloat16)
    terms[slots:, :] = jnp.zeros((padded - slots, width), jnp.bfloat16)

    tile = 512

    def up_step(k):
        weight_copies[k][0].wait()
        weight_copies[k][1].wait()
        blocks = toks[pl.ds(zs[k] * 4, 4)].reshape(every, width)
        rows_buf[...] = jnp.dot(
            pick[...], blocks, preferred_element_type=jnp.float32
        ).astype(jnp.bfloat16)

        @pl.loop(0, hidden // tile)
        def _(i):
            cols = pl.ds(pl.multiple_of(i * tile, tile), tile)
            rows = rows_buf[...]
            gate = jnp.dot(rows, gate_w[k, :, cols], preferred_element_type=jnp.float32)
            upper = jnp.dot(rows, up_w[k, :, cols], preferred_element_type=jnp.float32)
            if k > 0:
                gate = gate + gate_acc[:, cols]
                upper = upper + up_acc[:, cols]
            if k < 3:
                gate_acc[:, cols] = gate
                up_acc[:, cols] = upper
            else:
                hid[:, cols] = (gate / (1.0 + jnp.exp(-gate)) * upper).astype(jnp.bfloat16)

    def core_arrivals(k):
        for other in (core_e, diag_e):
            block = zs[k] * 4 + other
            arrival(toks.at[block], tok_recv.at[block])

    land_z(1)

    @pl.when(middle)
    def _():
        pass_on(1).start()
        land_z(2)
        pass_on(2).start()

    spread_z(1)
    forward_x(0)
    core_arrivals(0)
    up_step(0)

    @pl.when(middle)
    def _():
        land_z(3)
        pass_on(3).start()

    @pl.when(end)
    def _():
        land_z(2)

    spread_z(2)
    forward_x(1)
    core_arrivals(1)
    up_step(1)

    @pl.when(end)
    def _():
        land_z(3)

    spread_z(3)
    forward_x(2)
    core_arrivals(2)
    up_step(2)
    forward_x(3)
    core_arrivals(3)
    up_step(3)

    down_tile = 256

    def down_step(k):
        weight_copies[k][2].wait()

        @pl.loop(0, width // down_tile)
        def _(i):
            cols = pl.ds(pl.multiple_of(i * down_tile, down_tile), down_tile)
            product = jnp.dot(hid[...], down_w[k, :, cols], preferred_element_type=jnp.float32)
            terms[0:slots, cols] = (product * scale[:, 0:1]).astype(jnp.bfloat16)
            spread = jnp.dot(place[...], terms[:, cols], preferred_element_type=jnp.float32)
            outs[k, :, :, cols] = spread.astype(jnp.bfloat16).reshape(4, tok, down_tile)

        for i, there in enumerate((1 - x, x)):
            send(
                outs.at[k, 2 * there + 1 - c], core_in.at[k, i],
                rc_send.at[2 * k + i], rc_recv.at[2 * k + i], {"expert": core_e},
            )

    def core_step(k):
        arrival(core_in.at[k, 0], rc_recv.at[2 * k])
        x_out[k] = (
            outs[k, x_e].astype(jnp.float32) + core_in[k, 0].astype(jnp.float32)
        ).astype(jnp.bfloat16)
        send(x_out.at[k], x_in.at[k], rx_send.at[k], rx_recv.at[k], {"expert": x_e})

    def x_step(k):
        arrival(core_in.at[k, 1], rc_recv.at[2 * k + 1])
        arrival(x_in.at[k], rx_recv.at[k])
        total = (
            outs[k, e].astype(jnp.float32)
            + core_in[k, 1].astype(jnp.float32)
            + x_in[k].astype(jnp.float32)
        )
        if k == 0:
            return total

        def pass_sum(value, slot, there):
            z_out[k - 1] = value.astype(jnp.bfloat16)
            send(
                z_out.at[k - 1], z_in.at[slot], rz_send.at[k - 1], rz_recv.at[slot],
                {"tensor": there}, False,
            )

        @pl.when(end)
        def _():
            pass_sum(total, 3 - k, outer)

        @pl.when(middle)
        def _():
            pass_sum(total + landed(3 if k == 1 else 3 - k), 6 - k, outer if k == 1 else inner)

        return None

    def landed(slot):
        arrival(z_in.at[slot], rz_recv.at[slot])
        return z_in[slot].astype(jnp.float32)

    down_step(3)
    core_step(3)
    down_step(2)
    core_step(2)
    x_step(3)
    down_step(1)
    core_step(1)
    x_step(2)
    down_step(0)
    core_step(0)
    x_step(1)
    total = x_step(0)

    @pl.when(end)
    def _():
        out[...] = (total + landed(5)).astype(jnp.bfloat16)

    @pl.when(middle)
    def _():
        out[...] = (total + landed(2) + landed(4)).astype(jnp.bfloat16)
        pltpu.make_async_copy(tok_in, tok_in, z_send.at[1]).wait()
        for k in (1, 2, 3):
            pltpu.make_async_copy(tok_in, tok_in, z_send.at[k + 1]).wait()

    for k in (1, 2, 3):
        pltpu.make_async_copy(z_out.at[k - 1], z_out.at[k - 1], rz_send.at[k - 1]).wait()
    for copy in sends:
        copy.wait_send()


def per_device_fused(tokens, routes, gates, w_gate, w_up, w_down):
    tok, width = tokens.shape
    model, hidden = w_gate.shape[1:]
    experts = lax.axis_size("expert")
    slots = experts * CAP
    padded = (slots + 127) // 128 * 128
    every = experts * tok
    vmem = pl.BlockSpec(memory_space=pltpu.VMEM)
    hbm = pl.BlockSpec(memory_space=pl.ANY)
    bf, f32, dma = jnp.bfloat16, jnp.float32, pltpu.SemaphoreType.DMA
    return pl.pallas_call(
        layer_kernel,
        out_shape=jax.ShapeDtypeStruct((tok, width), bf),
        in_specs=[vmem, vmem, vmem, hbm, hbm, hbm],
        out_specs=vmem,
        scratch_shapes=[
            pltpu.VMEM((4 * experts, tok, width), bf),
            pltpu.VMEM((8, tok), f32),
            pltpu.VMEM((experts, 8, tok), f32),
            pltpu.VMEM((4, width, hidden), bf),
            pltpu.VMEM((4, width, hidden), bf),
            pltpu.VMEM((4, hidden, width), bf),
            pltpu.VMEM((slots, hidden), f32),
            pltpu.VMEM((slots, hidden), f32),
            pltpu.VMEM((slots, width), bf),
            pltpu.VMEM((slots, hidden), bf),
            pltpu.VMEM((slots, every), bf),
            pltpu.VMEM((every, padded), bf),
            pltpu.VMEM((slots, 128), f32),
            pltpu.VMEM((padded, width), bf),
            pltpu.VMEM((4, experts, tok, width), bf),
            pltpu.VMEM((4, 2, tok, width), bf),
            pltpu.VMEM((4, tok, width), bf),
            pltpu.VMEM((4, tok, width), bf),
            pltpu.VMEM((3, tok, width), bf),
            pltpu.VMEM((6, tok, width), bf),
            dma((12,)), dma((3,)), dma((experts,)), dma((5,)), dma((4,)), dma((8,)),
            dma((4 * experts,)),
            dma((8,)), dma((8,)), dma((4,)), dma((4,)), dma((3,)), dma((6,)),
        ],
        compiler_params=pltpu.CompilerParams(
            collective_id=0, has_side_effects=True, vmem_limit_bytes=62 * 1024 * 1024
        ),
        cost_estimate=pl.CostEstimate(
            flops=6 * slots * model * hidden,
            bytes_accessed=6 * model * hidden,
            transcendentals=slots * hidden,
        ),
    )(routes.T, gates.T, tokens, w_gate[0], w_up[0], w_down[0])


def solution(mesh):
    in_specs = (
        P(("groups", "expert"), "tensor"),
        P(("groups", "expert"), None),
        P(("groups", "expert"), None),
        P("expert", None, "tensor"),
        P("expert", None, "tensor"),
        P("expert", "tensor", None),
    )
    out_specs = P(("groups", "expert"), "tensor")
    fused = mesh.shape["tensor"] == 4 and mesh.shape["expert"] == 4
    return jax.shard_map(
        per_device_fused if fused else per_device,
        mesh=mesh, in_specs=in_specs, out_specs=out_specs, check_vma=False,
    )
```

```python
import jax
import jax.numpy as jnp
from jax import lax
from jax.experimental import pallas as pl
from jax.experimental.pallas import tpu as pltpu
from jax.sharding import PartitionSpec as P

CAP = 72
MESH = pl.DeviceIdType.MESH


row_tile = 128


def route_ranks(flat, experts):
    onehot = (flat[:, None] == jnp.arange(experts, dtype=jnp.int32)[None, :]).astype(jnp.int32)
    return jnp.sum((jnp.cumsum(onehot, axis=0) - 1) * onehot, axis=1)


def tile_terms(block, gate_panel, up_panel, down_panel):
    gate = jnp.dot(block, gate_panel, preferred_element_type=jnp.float32)
    upper = jnp.dot(block, up_panel, preferred_element_type=jnp.float32)
    hidden = (jax.nn.silu(gate) * upper).astype(jnp.bfloat16)
    return jnp.dot(hidden, down_panel, preferred_element_type=jnp.float32)


def expert_rows(rows, live, gate_panel, up_panel, down_panel):
    total = rows.shape[0]
    width = down_panel.shape[1]

    def step(index, acc):
        block = lax.dynamic_slice_in_dim(rows, index * row_tile, row_tile, 0)
        product = tile_terms(block, gate_panel, up_panel, down_panel)
        return lax.dynamic_update_slice_in_dim(acc, product, index * row_tile, 0)

    tiles = (live + row_tile - 1) // row_tile
    return lax.fori_loop(0, tiles, step, jnp.zeros((total, width), jnp.float32))


def compact_rows(arrived, incoming, offsets, padded):
    experts, capacity, width = arrived.shape
    position = jnp.arange(experts * capacity, dtype=jnp.int32)
    source = position // capacity
    within = position % capacity
    live_row = within < incoming[source]
    dest = jnp.where(live_row, offsets[source] + within, padded)
    flat_rows = arrived.reshape(experts * capacity, width)
    return jnp.zeros((padded, width), arrived.dtype).at[dest].set(flat_rows, mode="drop")


def per_device(tokens, routes, gates, w_gate, w_up, w_down):
    experts = lax.axis_size("expert")
    me = lax.axis_index("expert")
    tok = routes.shape[0]
    slice_width = tokens.shape[1]
    slots = experts * CAP
    padded = (slots + row_tile - 1) // row_tile * row_tile
    table = lax.all_gather(routes, "expert", axis=0, tiled=True)
    every_flat = table.reshape(-1)
    source_of = jnp.arange(every_flat.shape[0], dtype=jnp.int32) // (2 * tok)
    pair_index = source_of * experts + every_flat
    loads = jnp.sum(
        (pair_index[:, None] == jnp.arange(experts * experts, dtype=jnp.int32)[None, :]).astype(
            jnp.int32
        ),
        axis=0,
    ).reshape(experts, experts)
    flat = routes.reshape(-1)
    ranks = route_ranks(flat, experts)
    token_of = jnp.arange(2 * tok, dtype=jnp.int32) // 2
    incoming = loads[:, me]
    offsets = jnp.cumsum(incoming) - incoming
    live = jnp.sum(incoming)
    target = flat * CAP + ranks
    chosen = tokens[token_of]
    width = chosen.shape[1]
    outgoing = (
        jnp.zeros((slots, width), jnp.bfloat16)
        .at[target]
        .set(chosen, mode="drop")
        .reshape(experts, CAP, width)
    )
    arrived = lax.all_to_all(outgoing, "expert", split_axis=0, concat_axis=0, tiled=True)
    stacked = compact_rows(arrived, incoming, offsets, padded)
    stacked = lax.all_gather(stacked, "tensor", axis=1, tiled=True)
    terms = expert_rows(stacked, live, w_gate[0], w_up[0], w_down[0])
    summed = lax.psum_scatter(terms.astype(jnp.bfloat16), "tensor", scatter_dimension=1, tiled=True)
    position = jnp.arange(slots, dtype=jnp.int32)
    source = position // CAP
    within = position % CAP
    live_row = within < incoming[source]
    fetch = jnp.clip(offsets[source] + within, 0, padded - 1)
    restored = jnp.where(
        live_row[:, None], summed[fetch], jnp.zeros((slots, slice_width), jnp.bfloat16)
    )
    returned = lax.all_to_all(
        restored.reshape(experts, CAP, slice_width),
        "expert",
        split_axis=0,
        concat_axis=0,
        tiled=True,
    ).reshape(slots, slice_width)
    picked = returned[jnp.clip(target, 0, slots - 1)]
    weighted = picked.astype(jnp.float32).reshape(tok, 2, slice_width) * gates[:, :, None]
    return jnp.sum(weighted, axis=1).astype(jnp.bfloat16)


def near_to_far(z):
    half = z // 2
    return (z, z + 1 - 2 * (z % 2), 2 - half, 3 - 3 * half)


def layer_kernel(
    routes_in, gates_in, tok_in, gate_hbm, up_hbm, down_hbm, out,
    toks, meta_in, meta, gate_w, up_w, down_w, gate_acc, up_acc, rows_buf, hid, pick, place, scale, terms,
    outs, core_in, x_out, x_in, z_out, z_in,
    w_sem, meta_send, meta_recv, z_send, x_send, core_send, tok_recv,
    rc_send, rc_recv, rx_send, rx_recv, rz_send, rz_recv,
):
    e = lax.axis_index("expert")
    z = lax.axis_index("tensor")
    x = e // 2
    c = e % 2
    core_e = 2 * x + 1 - c
    x_e = 2 * (1 - x) + c
    diag_e = 2 * (1 - x) + 1 - c
    zs = near_to_far(z)
    outer, inner = zs[1], 3 - z
    middle = z % 3 > 0
    end = z % 3 == 0
    tok, width = tok_in.shape
    slots = pick.shape[0]
    every = pick.shape[1]
    hidden = hid.shape[1]

    named = lax.broadcasted_iota(jnp.int32, (8, tok), 0)
    meta_in[...] = jnp.where(routes_in[0:1, :] == named, gates_in[0:1, :], 0.0) + jnp.where(
        routes_in[1:2, :] == named, gates_in[1:2, :], 0.0
    )
    weight_copies = []
    for k in range(4):
        cut = pl.ds(pl.multiple_of(zs[k] * width, width), width)
        weight_copies.append(
            (
                pltpu.make_async_copy(gate_hbm.at[cut, :], gate_w.at[k], w_sem.at[k]),
                pltpu.make_async_copy(up_hbm.at[cut, :], up_w.at[k], w_sem.at[4 + k]),
                pltpu.make_async_copy(down_hbm.at[:, cut], down_w.at[k], w_sem.at[8 + k]),
            )
        )
    for k in range(4):
        weight_copies[k][0].start()
        weight_copies[k][1].start()
    for k in (3, 2, 1, 0):
        weight_copies[k][2].start()

    barrier = pltpu.get_barrier_semaphore()
    for other in (core_e, x_e, diag_e):
        pl.semaphore_signal(barrier, inc=1, device_id={"expert": other}, device_id_type=MESH)
    pl.semaphore_signal(barrier, inc=1, device_id={"tensor": outer}, device_id_type=MESH)

    @pl.when(middle)
    def _():
        pl.semaphore_signal(barrier, inc=1, device_id={"tensor": inner}, device_id_type=MESH)
        pl.semaphore_wait(barrier, 5)

    @pl.when(end)
    def _():
        pl.semaphore_wait(barrier, 4)


    sends = []

    def send(src, dst, s_sem, r_sem, where, keep=True):
        copy = pltpu.make_async_remote_copy(
            src_ref=src, dst_ref=dst, send_sem=s_sem, recv_sem=r_sem,
            device_id=where, device_id_type=MESH,
        )
        copy.start()
        if keep:
            sends.append(copy)
        return copy

    def arrival(ref, sem):
        pltpu.make_async_copy(ref, ref, sem).wait()

    for i, other in enumerate((x_e, core_e, diag_e)):
        send(meta_in, meta.at[e], meta_send.at[i], meta_recv.at[e], {"expert": other})
    half = tok // 2
    own = 2 * (z * 4 + e)

    def own_half(h):
        return tok_in.at[pl.ds(h * half, half)]

    for h in (0, 1):
        send(own_half(h), toks.at[own + h], x_send.at[h], tok_recv.at[own + h], {"expert": x_e})
        send(own_half(h), toks.at[own + h], z_send.at[h], tok_recv.at[own + h], {"tensor": outer})

        @pl.when(middle)
        def _():
            send(
                own_half(h), toks.at[own + h], z_send.at[2 + h], tok_recv.at[own + h],
                {"tensor": inner}, False,
            )

        send(own_half(h), toks.at[own + h], core_send.at[h], tok_recv.at[own + h], {"expert": core_e})
    toks[own] = tok_in[0:half, :]
    toks[own + 1] = tok_in[half:, :]
    meta[e] = meta_in[...]

    def piece_of(k, other, h):
        return 2 * (zs[k] * 4 + other) + h

    def land(k, other, h):
        piece = piece_of(k, other, h)
        arrival(toks.at[piece], tok_recv.at[piece])

    def hand_on(k, other, h, sem, where, keep=True):
        piece = piece_of(k, other, h)
        send(toks.at[piece], toks.at[piece], sem, tok_recv.at[piece], where, keep)

    def spread_z(k, h):
        hand_on(k, e, h, x_send.at[2 * k + h], {"expert": x_e})
        hand_on(k, e, h, core_send.at[2 * k + h], {"expert": core_e})

    def pass_on(k, h):
        hand_on(k, e, h, z_send.at[2 * (k + 1) + h], {"tensor": inner if k == 1 else outer}, False)

    def forward_x(k):
        for h in (0, 1):
            land(k, x_e, h)
            hand_on(k, x_e, h, core_send.at[8 + 2 * k + h], {"expert": core_e})

    for other in (x_e, core_e, diag_e):
        arrival(meta.at[other], meta_recv.at[other])

    own_row = lax.broadcasted_iota(jnp.int32, (8, tok), 0) == e
    weight = jnp.concatenate(
        [jnp.sum(jnp.where(own_row, meta[s], 0.0), axis=0, keepdims=True) for s in range(4)], axis=1
    )
    live = weight > 0.0
    ones = jnp.broadcast_to(jnp.where(live, 1.0, 0.0), (16, every)).astype(jnp.bfloat16)
    before = jnp.where(
        lax.broadcasted_iota(jnp.int32, (every, every), 0)
        < lax.broadcasted_iota(jnp.int32, (every, every), 1),
        1.0,
        0.0,
    ).astype(jnp.bfloat16)
    rank = jnp.dot(ones, before, preferred_element_type=jnp.float32)[0:1]
    key = jnp.where(live, rank, -1.0)
    row_hit = lax.broadcasted_iota(jnp.int32, (slots, every), 0).astype(jnp.float32) == key
    pick[...] = jnp.where(row_hit, 1.0, 0.0).astype(jnp.bfloat16)
    scale[...] = jnp.broadcast_to(
        jnp.sum(jnp.where(row_hit, weight, 0.0), axis=1, keepdims=True), scale.shape
    )
    column = jnp.transpose(jnp.broadcast_to(key, (128, every)))[:, 0:1]
    padded = place.shape[1]
    place[...] = jnp.where(
        lax.broadcasted_iota(jnp.int32, (every, padded), 1).astype(jnp.float32) == column, 1.0, 0.0
    ).astype(jnp.bfloat16)
    terms[slots:, :] = jnp.zeros((padded - slots, width), jnp.bfloat16)

    tile = 512

    def up_step(k):
        weight_copies[k][0].wait()
        weight_copies[k][1].wait()
        blocks = toks[pl.ds(zs[k] * 8, 8)].reshape(every, width)
        rows_buf[...] = jnp.dot(
            pick[...], blocks, preferred_element_type=jnp.float32
        ).astype(jnp.bfloat16)

        @pl.loop(0, hidden // tile)
        def _(i):
            cols = pl.ds(pl.multiple_of(i * tile, tile), tile)
            rows = rows_buf[...]
            gate = jnp.dot(rows, gate_w[k, :, cols], preferred_element_type=jnp.float32)
            upper = jnp.dot(rows, up_w[k, :, cols], preferred_element_type=jnp.float32)
            if k > 0:
                gate = gate + gate_acc[:, cols]
                upper = upper + up_acc[:, cols]
            if k < 3:
                gate_acc[:, cols] = gate
                up_acc[:, cols] = upper
            else:
                hid[:, cols] = (gate / (1.0 + jnp.exp(-gate)) * upper).astype(jnp.bfloat16)

    def core_arrivals(k):
        for other in (core_e, diag_e):
            for h in (0, 1):
                land(k, other, h)

    def relay(k, passing):
        for h in (0, 1):
            land(k, e, h)
            if passing:
                pass_on(k, h)

    for h in (0, 1):
        land(1, e, h)

        @pl.when(middle)
        def _():
            pass_on(1, h)

        spread_z(1, h)

    @pl.when(middle)
    def _():
        relay(2, True)

    forward_x(0)
    core_arrivals(0)
    up_step(0)
    for h in (0, 1):

        @pl.when(end)
        def _():
            land(2, e, h)

        spread_z(2, h)

    @pl.when(middle)
    def _():
        relay(3, True)

    forward_x(1)
    core_arrivals(1)
    up_step(1)
    for h in (0, 1):

        @pl.when(end)
        def _():
            land(3, e, h)

        spread_z(3, h)

    forward_x(2)
    core_arrivals(2)
    up_step(2)
    forward_x(3)
    core_arrivals(3)
    up_step(3)

    down_tile = 256

    def down_step(k):
        weight_copies[k][2].wait()

        @pl.loop(0, width // down_tile)
        def _(i):
            cols = pl.ds(pl.multiple_of(i * down_tile, down_tile), down_tile)
            product = jnp.dot(hid[...], down_w[k, :, cols], preferred_element_type=jnp.float32)
            terms[0:slots, cols] = (product * scale[:, 0:1]).astype(jnp.bfloat16)
            spread = jnp.dot(place[...], terms[:, cols], preferred_element_type=jnp.float32)
            outs[k, :, :, cols] = spread.astype(jnp.bfloat16).reshape(4, tok, down_tile)

        for i, there in enumerate((1 - x, x)):
            send(
                outs.at[k, 2 * there + 1 - c], core_in.at[k, i],
                rc_send.at[2 * k + i], rc_recv.at[2 * k + i], {"expert": core_e},
            )

    def cut(h):
        return pl.ds(h * half, half)

    def wide(value):
        return value.astype(jnp.float32)

    def core_step(k):
        arrival(core_in.at[k, 0], rc_recv.at[2 * k])
        for h in (0, 1):
            x_out[k, cut(h)] = (wide(outs[k, x_e, cut(h)]) + wide(core_in[k, 0, cut(h)])).astype(
                jnp.bfloat16
            )
            send(
                x_out.at[k, cut(h)], x_in.at[k, cut(h)], rx_send.at[2 * k + h],
                rx_recv.at[2 * k + h], {"expert": x_e},
            )

    def landed(slot, h):
        arrival(z_in.at[slot, cut(h)], rz_recv.at[2 * slot + h])
        return wide(z_in[slot, cut(h)])

    def x_step(k):
        arrival(core_in.at[k, 1], rc_recv.at[2 * k + 1])
        for h in (0, 1):
            arrival(x_in.at[k, cut(h)], rx_recv.at[2 * k + h])
            total = (
                wide(outs[k, e, cut(h)]) + wide(core_in[k, 1, cut(h)]) + wide(x_in[k, cut(h)])
            )

            def pass_sum(value, slot, there):
                z_out[k - 1, cut(h)] = value.astype(jnp.bfloat16)
                send(
                    z_out.at[k - 1, cut(h)], z_in.at[slot, cut(h)], rz_send.at[2 * (k - 1) + h],
                    rz_recv.at[2 * slot + h], {"tensor": there}, False,
                )

            @pl.when(end)
            def _():
                if k == 0:
                    out[cut(h), :] = (total + landed(5, h)).astype(jnp.bfloat16)
                else:
                    pass_sum(total, 3 - k, outer)

            @pl.when(middle)
            def _():
                if k == 0:
                    out[cut(h), :] = (total + landed(2, h) + landed(4, h)).astype(jnp.bfloat16)
                else:
                    pass_sum(
                        total + landed(3 if k == 1 else 3 - k, h), 6 - k, outer if k == 1 else inner
                    )

    down_step(3)
    down_step(2)
    core_step(3)
    down_step(1)
    core_step(2)
    x_step(3)
    down_step(0)
    core_step(1)
    core_step(0)
    x_step(2)
    x_step(1)
    x_step(0)

    @pl.when(middle)
    def _():
        for i in range(2, 10):
            pltpu.make_async_copy(own_half(0), own_half(0), z_send.at[i]).wait()

    for i in range(6):
        sent = z_out.at[i // 2, cut(i % 2)]
        pltpu.make_async_copy(sent, sent, rz_send.at[i]).wait()

    for copy in sends:
        copy.wait_send()


def per_device_fused(tokens, routes, gates, w_gate, w_up, w_down):
    tok, width = tokens.shape
    model, hidden = w_gate.shape[1:]
    experts = lax.axis_size("expert")
    slots = experts * CAP
    padded = (slots + 127) // 128 * 128
    every = experts * tok
    vmem = pl.BlockSpec(memory_space=pltpu.VMEM)
    hbm = pl.BlockSpec(memory_space=pl.ANY)
    bf, f32, dma = jnp.bfloat16, jnp.float32, pltpu.SemaphoreType.DMA
    return pl.pallas_call(
        layer_kernel,
        out_shape=jax.ShapeDtypeStruct((tok, width), bf),
        in_specs=[vmem, vmem, vmem, hbm, hbm, hbm],
        out_specs=vmem,
        scratch_shapes=[
            pltpu.VMEM((8 * experts, tok // 2, width), bf),
            pltpu.VMEM((8, tok), f32),
            pltpu.VMEM((experts, 8, tok), f32),
            pltpu.VMEM((4, width, hidden), bf),
            pltpu.VMEM((4, width, hidden), bf),
            pltpu.VMEM((4, hidden, width), bf),
            pltpu.VMEM((slots, hidden), f32),
            pltpu.VMEM((slots, hidden), f32),
            pltpu.VMEM((slots, width), bf),
            pltpu.VMEM((slots, hidden), bf),
            pltpu.VMEM((slots, every), bf),
            pltpu.VMEM((every, padded), bf),
            pltpu.VMEM((slots, 128), f32),
            pltpu.VMEM((padded, width), bf),
            pltpu.VMEM((4, experts, tok, width), bf),
            pltpu.VMEM((4, 2, tok, width), bf),
            pltpu.VMEM((4, tok, width), bf),
            pltpu.VMEM((4, tok, width), bf),
            pltpu.VMEM((3, tok, width), bf),
            pltpu.VMEM((6, tok, width), bf),
            dma((12,)), dma((3,)), dma((experts,)), dma((10,)), dma((8,)), dma((16,)),
            dma((8 * experts,)),
            dma((8,)), dma((8,)), dma((8,)), dma((8,)), dma((6,)), dma((12,)),
        ],
        compiler_params=pltpu.CompilerParams(
            collective_id=0, has_side_effects=True, vmem_limit_bytes=62 * 1024 * 1024
        ),
        cost_estimate=pl.CostEstimate(
            flops=6 * slots * model * hidden,
            bytes_accessed=6 * model * hidden,
            transcendentals=slots * hidden,
        ),
    )(routes.T, gates.T, tokens, w_gate[0], w_up[0], w_down[0])


def solution(mesh):
    in_specs = (
        P(("groups", "expert"), "tensor"),
        P(("groups", "expert"), None),
        P(("groups", "expert"), None),
        P("expert", None, "tensor"),
        P("expert", None, "tensor"),
        P("expert", "tensor", None),
    )
    out_specs = P(("groups", "expert"), "tensor")
    fused = mesh.shape["tensor"] == 4 and mesh.shape["expert"] == 4
    return jax.shard_map(
        per_device_fused if fused else per_device,
        mesh=mesh, in_specs=in_specs, out_specs=out_specs, check_vma=False,
    )
```
